32 devices in a mesh: dp: 4 (over x, core), ctx: 8 (over z, y).
Axes of the slice: x: 2, y: 2, z: 4, core: 2. Of those that a mesh axis runs over, the one named last changes fastest.
Arguments:
- queries: bfloat16 [4, 1024, 2048], P('dp', 'ctx'), may hold values from -150 to 150
- key_rows: bfloat16 [4, 1024, 512], P('dp', 'ctx'), may hold values from -5 to 5
- value_rows: bfloat16 [4, 1024, 512], P('dp', 'ctx'), may hold values from -6 to 6
- cotangent: bfloat16 [4, 1024, 2048], P('dp', 'ctx'), may hold values from -6 to 6
- sink_logits: float32 [16], replicated, may hold values from -1 to 3
- run_lengths: int32 [4, 3], P('dp'), may hold values from 1 to 4, 8 in all within a row
- segment_ids: int32 [4, 1024], P('dp', 'ctx'), may hold values from 0 to 3, never falling along the last dimension, each value on 1 to 512 neighbouring positions
Outputs:
- attended: bfloat16 [4, 1024, 2048], P('dp', 'ctx')
- grad_queries: bfloat16 [4, 1024, 2048], P('dp', 'ctx')
- grad_keys: bfloat16 [4, 1024, 512], P('dp', 'ctx')
- grad_values: bfloat16 [4, 1024, 512], P('dp', 'ctx')
- grad_sink: float32 [16], replicated
The draws below stay inside these ranges and needn't reach their ends.
Inputs may be any that keep to these rules, and one draw needn't show every extreme that they name: `run_lengths`: in each sequence the trajectories cover all shards in order; each spans 1 to 4 shards and one spans exactly 4. `segment_ids`: never falls along a sequence; each episode spans 1 to 512 tokens and one spans exactly 512.
All inputs are finite; a program needn't handle non-finite values.
Results may differ from the reference program's by a relative error of at most 0.04.
Values may be sent and summed in bfloat16 or wider, within the bound.
A program may use at most 64 MiB of HBM per device.

```python
import math
import jax
import jax.numpy as jnp
import numpy as np
from jax import lax

HEADS = 16
KV_HEADS = 4
HEAD_DIM = 128
TOK_DEV = 128
BATCH = 4
SEQ = 1024
MOST = 4
RUNS = 3
SEG_MOST = 512
SEG_COUNT = 4
N_CTX = 8


def draw_key_rows(key, part):
    drawn_draw = jax.random.normal(jax.random.fold_in(key, 21), (BATCH, SEQ, KV_HEADS * HEAD_DIM), jnp.float32)
    return jnp.clip(drawn_draw, -5.0, 5.0).astype(jnp.bfloat16)


def draw_queries(key, part):
    group_size = HEADS // KV_HEADS
    base_draw = jnp.clip(jax.random.normal(jax.random.fold_in(key, 31), (BATCH, SEQ, KV_HEADS, group_size, HEAD_DIM), jnp.float32), -5.0, 5.0)
    return base_draw.reshape(BATCH, SEQ, HEADS * HEAD_DIM).astype(jnp.bfloat16)


def shard_levels(rng, shape, cuts, low, high):
    gain = 1.0
    for position, parts in cuts:
        draws = jax.random.uniform(jax.random.fold_in(jax.random.fold_in(rng, 6), position), (parts,), jnp.float32, low / len(cuts), high / len(cuts))
        gain = gain * jnp.repeat(jnp.exp(draws), shape[position] // parts).reshape((-1,) + (1,) * (len(shape) - 1 - position))
    return gain


def split_up(count, total, limit, slope):
    weights = [(1 << 20) // math.isqrt(standing ** slope) + 1 for standing in range(2, count + 1)]
    rest, given = total - limit - (count - 1), [1] * (count - 1)
    while rest > 0:
        free = [i for i in range(count - 1) if given[i] < limit]
        mass, left = sum([weights[i] for i in free]), rest
        for i in free:
            addition = min(limit - given[i], max(1, left * weights[i] // mass), rest)
            given[i] = given[i] + addition
            rest = rest - addition
    return np.array([limit] + given)


def uneven(key, amount, total, bound, skew):
    if amount == 2:
        one = jax.random.randint(key, (), max(1, total - bound), min(bound, total - 1) + 1)
        return jnp.stack([one, total - one])
    sizes = jnp.asarray(split_up(amount, total, bound, skew), jnp.int32)
    pairs = (amount - 1) // 2
    giver, sink = sizes[1:1 + 2 * pairs:2], sizes[2:2 + 2 * pairs:2]
    room = jnp.minimum(giver - 1, bound - sink)
    moved = jax.random.randint(jax.random.fold_in(key, 1), (pairs,), 0, 1 << 20) % (room + 1)
    sizes = sizes.at[1:1 + 2 * pairs:2].set(giver - moved).at[2:2 + 2 * pairs:2].set(sink + moved)
    return sizes[jax.random.permutation(jax.random.fold_in(key, 2), amount)]


def normal_values(key, shape, deviation, reach, pieces=(), kind=jnp.bfloat16):
    gain = shard_levels(key, shape, pieces, -0.22, 0.18) if pieces else 1.0
    entries = jax.random.normal(key, shape, jnp.float32) * deviation * gain
    return jnp.minimum(jnp.maximum(entries, -reach), reach).astype(kind)


def setup_inputs(seed: int = 0) -> dict:
    arg_keys = jax.random.split(jax.random.key(seed), 8)
    return {
        "queries": draw_queries(jax.random.fold_in(arg_keys[7], 71), 0),
        "key_rows": draw_key_rows(jax.random.fold_in(arg_keys[7], 71), 0),
        "value_rows": normal_values(arg_keys[2], (BATCH, SEQ, KV_HEADS * HEAD_DIM), 1.0, 6.0, ((0, 4), (1, 8))),
        "cotangent": normal_values(arg_keys[3], (BATCH, SEQ, HEADS * HEAD_DIM), 1.0, 6.0, ((0, 4), (1, 8))),
        "sink_logits": jnp.clip(jax.random.uniform(arg_keys[4], (HEADS,), jnp.float32, -1.0, 3.0), -1.0, 3.0),
        "run_lengths": jax.vmap(lambda own: uneven(own, RUNS, N_CTX, MOST, 2))(jax.random.split(arg_keys[5], BATCH)).reshape((BATCH, RUNS)).astype(jnp.int32),
        "segment_ids": jax.vmap(lambda own: jnp.searchsorted(jnp.cumsum(uneven(own, SEG_COUNT, SEQ, SEG_MOST, 2)), jnp.arange(SEQ), side="right"))(jax.random.split(arg_keys[6], BATCH)).reshape((BATCH, SEQ)).astype(jnp.int32),
    }


def traj_index(run_ends, shard_index):
    return lax.optimization_barrier(jnp.sum((run_ends[None, :] <= shard_index[:, None]).astype(jnp.int32), axis=1))

def head_block(query_heads, key_win, value_win, grad_heads, allowed, sink_part, factor):
    query_f = query_heads.astype(jnp.float32)
    key_f = key_win.astype(jnp.float32)
    value_f = value_win.astype(jnp.float32)
    grad_f = grad_heads.astype(jnp.float32)
    scores = jnp.einsum('rgd,wd->grw', query_f, key_f) * factor
    scores = jnp.where(allowed[None], scores, -jnp.inf)
    row_top = jnp.maximum(lax.optimization_barrier(jnp.max(scores, axis=2)), sink_part[:, None])
    exp_terms = jnp.exp(scores - row_top[:, :, None])
    sink_exp = jnp.exp(sink_part[:, None] - row_top)
    denominator = lax.optimization_barrier(jnp.sum(exp_terms, axis=2)) + sink_exp
    weights = exp_terms / denominator[:, :, None]
    weights_low = weights.astype(jnp.bfloat16)
    attended = jnp.einsum('grw,wd->rgd', weights_low.astype(jnp.float32), value_f).astype(jnp.bfloat16)
    row_dot = lax.optimization_barrier(jnp.sum(grad_f * attended.astype(jnp.float32), axis=2)).T
    grad_weights = jnp.einsum('rgd,wd->grw', grad_f, value_f)
    grad_scores = (weights * (grad_weights - row_dot[:, :, None])).astype(jnp.bfloat16)
    grad_scores_f = grad_scores.astype(jnp.float32)
    grad_query = (jnp.einsum('grw,wd->rgd', grad_scores_f, key_f) * factor).astype(jnp.bfloat16)
    grad_key = jnp.einsum('grw,rgd->wd', grad_scores_f, query_f) * factor
    grad_value = jnp.einsum('grw,rgd->wd', weights_low.astype(jnp.float32), grad_f)
    grad_sink = -lax.optimization_barrier(jnp.sum(sink_exp / denominator * row_dot, axis=1))
    return (attended, grad_query, grad_key, grad_value, grad_sink)

def reference(queries, key_rows, value_rows, cotangent, sink_logits, run_lengths, segment_ids):
    group_size = HEADS // KV_HEADS
    factor = HEAD_DIM ** (-0.5)
    pad_rows = (MOST - 1) * TOK_DEV
    span_rows = MOST * TOK_DEV
    kv_width = KV_HEADS * HEAD_DIM

    def one_sequence(packed):
        query_seq, key_seq, value_seq, grad_seq, lengths, seg_seq = packed
        run_ends = jnp.cumsum(lengths).astype(jnp.int32)
        key_pad = jnp.concatenate([jnp.zeros((pad_rows, kv_width), key_seq.dtype), key_seq], 0)
        value_pad = jnp.concatenate([jnp.zeros((pad_rows, kv_width), value_seq.dtype), value_seq], 0)
        seg_pad = jnp.concatenate([jnp.full((pad_rows,), -1, jnp.int32), seg_seq.astype(jnp.int32)], 0)

        def visit_shard(carried, shard_index):
            key_acc, value_acc = carried
            start_row = (shard_index * TOK_DEV).astype(jnp.int32)
            query_blk = lax.dynamic_slice_in_dim(query_seq, start_row, TOK_DEV, 0)
            grad_blk = lax.dynamic_slice_in_dim(grad_seq, start_row, TOK_DEV, 0)
            seg_query = lax.dynamic_slice_in_dim(seg_seq.astype(jnp.int32), start_row, TOK_DEV, 0)
            key_win = lax.dynamic_slice_in_dim(key_pad, start_row, span_rows, 0)
            value_win = lax.dynamic_slice_in_dim(value_pad, start_row, span_rows, 0)
            seg_win = lax.dynamic_slice_in_dim(seg_pad, start_row, span_rows, 0)
            columns = jnp.arange(span_rows, dtype=jnp.int32)
            key_shard = shard_index - MOST + 1 + columns // TOK_DEV
            key_pos = key_shard * TOK_DEV + columns % TOK_DEV
            query_pos = start_row + jnp.arange(TOK_DEV, dtype=jnp.int32)
            my_traj = jnp.sum((run_ends <= shard_index).astype(jnp.int32))
            allowed = ((key_shard >= 0) & (traj_index(run_ends, key_shard) == my_traj))[None, :] & (seg_win[None, :] == seg_query[:, None]) & (key_pos[None, :] <= query_pos[:, None])
            outs_list = [[], [], [], [], []]
            for kv_head in range(KV_HEADS):
                query_cols = slice(kv_head * group_size * HEAD_DIM, (kv_head + 1) * group_size * HEAD_DIM)
                key_cols = slice(kv_head * HEAD_DIM, (kv_head + 1) * HEAD_DIM)
                head_parts = head_block(query_blk[:, query_cols].reshape(TOK_DEV, group_size, HEAD_DIM), key_win[:, key_cols], value_win[:, key_cols], grad_blk[:, query_cols].reshape(TOK_DEV, group_size, HEAD_DIM), allowed, sink_logits[kv_head * group_size:(kv_head + 1) * group_size], factor)
                for member in range(5):
                    outs_list[member].append(head_parts[member])
            attended = jnp.concatenate([block_out.reshape(TOK_DEV, -1) for block_out in outs_list[0]], 1)
            grad_query = jnp.concatenate([block_out.reshape(TOK_DEV, -1) for block_out in outs_list[1]], 1)
            grad_key = jnp.concatenate(outs_list[2], 1)
            grad_value = jnp.concatenate(outs_list[3], 1)
            grad_sink = jnp.concatenate(outs_list[4], 0)
            key_old = lax.dynamic_slice_in_dim(key_acc, start_row, span_rows, 0).astype(jnp.float32)
            value_old = lax.dynamic_slice_in_dim(value_acc, start_row, span_rows, 0).astype(jnp.float32)
            key_acc = lax.dynamic_update_slice_in_dim(key_acc, (key_old + grad_key).astype(jnp.bfloat16), start_row, 0)
            value_acc = lax.dynamic_update_slice_in_dim(value_acc, (value_old + grad_value).astype(jnp.bfloat16), start_row, 0)
            return ((key_acc, value_acc), (attended, grad_query, grad_sink))
        zeros_acc = jnp.zeros((pad_rows + SEQ, kv_width), jnp.bfloat16)
        order = (N_CTX - 1 - jnp.arange(N_CTX, dtype=jnp.int32)).astype(jnp.int32)
        (key_acc, value_acc), (attended, grad_query, grad_sink) = lax.scan(visit_shard, (zeros_acc, zeros_acc), order)
        return (attended[::-1].reshape(SEQ, -1), grad_query[::-1].reshape(SEQ, -1), key_acc[pad_rows:], value_acc[pad_rows:], lax.optimization_barrier(jnp.sum(grad_sink, axis=0)))
    attended, grad_queries, grad_keys, grad_values, sink_parts = lax.map(one_sequence, (queries, key_rows, value_rows, cotangent, run_lengths, segment_ids))
    grad_sink = lax.optimization_barrier(jnp.sum(sink_parts, axis=0)) / math.sqrt(BATCH * SEQ)
    return (attended, grad_queries, grad_keys, grad_values, grad_sink)
```

```python
import functools
import math

import jax
import jax.numpy as jnp
from jax import lax
from jax.experimental import pallas as pl
from jax.experimental.pallas import tpu as pltpu
from jax.sharding import PartitionSpec as P

HEADS = 16
KV_HEADS = 4
HEAD_DIM = 128
GROUP = HEADS // KV_HEADS
LOG2E = math.log2(math.e)
AWAY = -1e30
MESH = pl.DeviceIdType.MESH


def edge_lists(most):
    edges = {0: [], 1: []}
    for parity in (0, 1):
        for kept in range(1, most):
            if parity == 0:
                step = -1 if kept == 1 and most > 2 else min(kept, 2)
            else:
                step = {1: 1, 2: 2, 3: 1}.get(kept, 2)
            sender = parity if step % 2 == 0 else 1 - parity
            edges[sender].append((kept - step, step, kept))
    return edges


def levels(edges, most):
    depth = {(0, 0): 0, (1, 0): 0}
    while len(depth) < 2 * most:
        for parity in (0, 1):
            for held, step, kept in edges[parity]:
                if (parity, held) in depth:
                    depth[((parity + step) % 2, kept)] = depth[(parity, held)] + 1
    return depth


def kernel(
    n_dp, n_ctx, most,
    sink_ref, runs_ref, q_ref, k_ref, v_ref, do_ref, seg_ref,
    att_ref, dq_ref, dk_ref, dv_ref, dsink_ref,
    kv, gsum, gout, gin, segs, bias, sink_rows, ctx_rows, dp_rows,
    f_send, f_recv, b_send, b_recv, s_send, s_recv, c_send, c_recv, d_send, d_recv,
):
    tok = k_ref.shape[1]
    me = lax.axis_index("ctx")
    my_dp = lax.axis_index("dp")
    odd = lax.rem(me, 2)
    edges = edge_lists(most)
    depth = levels(edges, most)
    deepest = max(depth.values())
    factor = HEAD_DIM ** (-0.5)

    barrier = pltpu.get_barrier_semaphore()
    for j in range(1, n_ctx):
        pl.semaphore_signal(barrier, inc=1, device_id={"ctx": lax.rem(me + j, n_ctx)}, device_id_type=MESH)
    for j in range(1, n_dp):
        pl.semaphore_signal(barrier, inc=1, device_id={"dp": lax.rem(my_dp + j, n_dp)}, device_id_type=MESH)
    for h in range(KV_HEADS):
        cols = slice(h * HEAD_DIM, (h + 1) * HEAD_DIM)
        kv[h, 0, 0:tok, :] = k_ref[0, :, cols]
        kv[h, 1, 0:tok, :] = v_ref[0, :, cols]
    segs[0] = seg_ref[...]
    pl.semaphore_wait(barrier, n_ctx - 1 + n_dp - 1)

    def rows(dist):
        return pl.ds(dist * tok, tok)

    def forward(h, parity, index):
        held, step, kept = edges[parity][index]
        return pltpu.make_async_remote_copy(
            src_ref=kv.at[h, :, rows(held)],
            dst_ref=kv.at[h, :, rows(kept)],
            send_sem=f_send.at[h, index],
            recv_sem=f_recv.at[h, kept],
            device_id={"ctx": me + step},
            device_id_type=MESH,
        )

    def backward(h, kept, parity, index):
        held, step, k = edges[parity][index]
        return pltpu.make_async_remote_copy(
            src_ref=gout.at[h, :, rows(kept)],
            dst_ref=gin.at[h, index],
            send_sem=b_send.at[h, kept],
            recv_sem=b_recv.at[h, index],
            device_id={"ctx": me - step},
            device_id_type=MESH,
        )

    def edge_live(held, step):
        return (me >= held) & (me + step >= 0) & (me + step < n_ctx)

    def start_forward(h, level):
        for parity in (0, 1):
            for index, (held, step, kept) in enumerate(edges[parity]):
                if depth[(parity, held)] == level:
                    @pl.when((odd == parity) & edge_live(held, step))
                    def _():
                        forward(h, parity, index).start()

    def wait_forward(h, level):
        for kept in range(1, most):
            for parity in (0, 1):
                if depth[(parity, kept)] == level:
                    @pl.when((odd == parity) & (me >= kept))
                    def _():
                        pltpu.make_async_remote_copy(
                            src_ref=kv.at[h, :, rows(kept)],
                            dst_ref=kv.at[h, :, rows(kept)],
                            send_sem=f_send.at[h, 0],
                            recv_sem=f_recv.at[h, kept],
                            device_id={"ctx": lax.rem(me + 1, n_ctx)},
                            device_id_type=MESH,
                        ).wait_recv()

    def parent_edge(parity, kept):
        for p in (0, 1):
            for index, (held, step, k) in enumerate(edges[p]):
                if k == kept and (p + step) % 2 == parity:
                    return p, index

    def child_level(parity, held):
        below = [
            child_level((parity + step) % 2, kept) + 1
            for h0, step, kept in edges[parity] if h0 == held
        ]
        return max(below, default=0)

    def back_step(h, level):
        for parity in (0, 1):
            for held in range(most):
                if child_level(parity, held) != level:
                    continue
                for index, (h0, step, kept) in enumerate(edges[parity]):
                    if h0 == held:
                        @pl.when((odd == parity) & edge_live(held, step))
                        def _():
                            pltpu.make_async_remote_copy(
                                src_ref=gin.at[h, index],
                                dst_ref=gin.at[h, index],
                                send_sem=b_send.at[h, 0],
                                recv_sem=b_recv.at[h, index],
                                device_id={"ctx": lax.rem(me + 1, n_ctx)},
                                device_id_type=MESH,
                            ).wait_recv()
                            gsum[h, :, rows(held)] += gin[h, index].astype(jnp.float32)
                if held == 0:
                    @pl.when(odd == parity)
                    def _():
                        cols = slice(h * HEAD_DIM, (h + 1) * HEAD_DIM)
                        dk_ref[0, :, cols] = gsum[h, 0, 0:tok].astype(dk_ref.dtype)
                        dv_ref[0, :, cols] = gsum[h, 1, 0:tok].astype(dv_ref.dtype)
                else:
                    p, index = parent_edge(parity, held)
                    @pl.when((odd == parity) & (me >= held))
                    def _():
                        gout[h, :, rows(held)] = gsum[h, :, rows(held)].astype(gout.dtype)
                        backward(h, held, p, index).start()

    def seg_copy(dist):
        return pltpu.make_async_remote_copy(
            src_ref=segs.at[0], dst_ref=segs.at[dist],
            send_sem=s_send.at[dist], recv_sem=s_recv.at[dist],
            device_id={"ctx": me + dist}, device_id_type=MESH,
        )

    for dist in range(1, most):
        @pl.when(me + dist < n_ctx)
        def _():
            seg_copy(dist).start()
    for h in range(KV_HEADS):
        start_forward(h, 0)

    for dist in range(1, most):
        @pl.when(me < dist)
        def _():
            kv[:, :, rows(dist), :] = jnp.zeros((KV_HEADS, 2, tok, HEAD_DIM), kv.dtype)
            segs[dist] = jnp.full(segs.shape[1:], -1, segs.dtype)

    for dist in range(1, most):
        @pl.when(me >= dist)
        def _():
            seg_copy(dist).wait_recv()

    def traj(shard):
        end, count = 0, 0
        for i in range(runs_ref.shape[1]):
            end = end + runs_ref[0, i]
            count = count + jnp.where(end <= shard, 1, 0)
        return count

    mine = traj(me)
    seg_query = jnp.broadcast_to(segs[0], (tok, tok))
    for dist in range(most):
        seg_key = jnp.transpose(jnp.broadcast_to(segs[dist], (tok, tok)).astype(jnp.float32))
        level = jnp.where((traj(me - dist) == mine) & (me >= dist), 0.0, AWAY)
        allowed = seg_key == seg_query.astype(jnp.float32)
        if dist == 0:
            key_pos = lax.broadcasted_iota(jnp.int32, (tok, tok), 0)
            query_pos = lax.broadcasted_iota(jnp.int32, (tok, tok), 1)
            allowed = allowed & (key_pos <= query_pos)
        bias[rows(dist), :] = jnp.where(allowed, level, AWAY)

    def nn(a, b):
        return jnp.dot(a, b, preferred_element_type=jnp.float32)

    def compute(h):
        heads = [h * GROUP + g for g in range(GROUP)]
        keys, values = kv[h, 0], kv[h, 1]
        keys_t, values_t = keys.T, values.T
        gk = gv = None
        for g in range(GROUP):
            cols = slice(heads[g] * HEAD_DIM, (heads[g] + 1) * HEAD_DIM)
            q = q_ref[0, :, cols]
            do = do_ref[0, :, cols]
            do_t = do.T
            scores = nn(keys, q.T) * (factor * LOG2E) + bias[...]
            sink = sink_ref[heads[g]] * LOG2E
            top = jnp.maximum(jnp.max(scores, axis=0, keepdims=True), sink)
            terms = jnp.exp2(scores - top)
            sink_exp = jnp.exp2(sink - top)
            denom = jnp.sum(terms, axis=0, keepdims=True) + sink_exp
            inv = 1.0 / denom
            weights = terms * inv
            low = weights.astype(jnp.bfloat16)
            att = nn(values_t, low).astype(jnp.bfloat16)
            att_ref[0, :, cols] = att.T
            row_dot = jnp.sum(att.astype(jnp.float32) * do_t.astype(jnp.float32), axis=0, keepdims=True)
            gw = nn(values, do_t)
            gs = (weights * (gw - row_dot)).astype(jnp.bfloat16)
            gq = nn(keys_t, gs) * factor
            dq_ref[0, :, cols] = gq.astype(jnp.bfloat16).T
            new_k, new_v = nn(gs, q), nn(low, do)
            gk = new_k if gk is None else gk + new_k
            gv = new_v if gv is None else gv + new_v
            sink_rows[pl.ds(heads[g], 1), :] = -(sink_exp * inv * row_dot)
        gsum[h, 0] = gk * factor
        gsum[h, 1] = gv

    def run_forward(upto):
        for h, level in upto:
            wait_forward(h, level)
            if level < deepest:
                start_forward(h, level)

    order = sorted(
        ((h, level) for h in range(KV_HEADS) for level in range(1, deepest + 1)),
        key=lambda item: (item[0] + item[1], item[0]),
    )
    done = 0
    back_deepest = max(child_level(p, k) for p in (0, 1) for k in range(most))
    pending = []
    for h in range(KV_HEADS):
        last = order.index((h, deepest)) + 1
        run_forward(order[done:last])
        done = max(done, last)
        compute(h)
        back_step(h, 0)
        for other in range(h):
            level = h - other
            if level <= back_deepest:
                back_step(other, level)
                pending.append((other, level))

    padded = jnp.concatenate(
        [sink_rows[...], jnp.zeros((128 - HEADS, tok), jnp.float32)], 0
    )
    ctx_rows[me] = jnp.sum(padded.T, axis=0, keepdims=True)

    def ctx_copy(j):
        return pltpu.make_async_remote_copy(
            src_ref=ctx_rows.at[me], dst_ref=ctx_rows.at[me],
            send_sem=c_send.at[j], recv_sem=c_recv.at[me],
            device_id={"ctx": lax.rem(me + j, n_ctx)}, device_id_type=MESH,
        )

    def dp_copy(j):
        return pltpu.make_async_remote_copy(
            src_ref=dp_rows.at[my_dp], dst_ref=dp_rows.at[my_dp],
            send_sem=d_send.at[j], recv_sem=d_recv.at[my_dp],
            device_id={"dp": lax.rem(my_dp + j, n_dp)}, device_id_type=MESH,
        )

    for j in range(1, n_ctx):
        ctx_copy(j).start()

    rest = sorted(
        ((h, level) for h in range(KV_HEADS) for level in range(1, back_deepest + 1)
         if (h, level) not in pending),
        key=lambda item: (item[0] + item[1], item[0]),
    )
    half = [item for item in rest if item != (KV_HEADS - 1, back_deepest)]
    for h, level in half:
        back_step(h, level)

    for j in range(1, n_ctx):
        other = lax.rem(me + j, n_ctx)
        pltpu.make_async_remote_copy(
            src_ref=ctx_rows.at[other], dst_ref=ctx_rows.at[other],
            send_sem=c_send.at[j], recv_sem=c_recv.at[other],
            device_id={"ctx": other}, device_id_type=MESH,
        ).wait_recv()
    total = ctx_rows[0]
    for j in range(1, n_ctx):
        total = total + ctx_rows[j]
    dp_rows[my_dp] = total
    for j in range(1, n_dp):
        dp_copy(j).start()

    for item in rest:
        if item not in half:
            back_step(*item)

    for j in range(1, n_dp):
        other = lax.rem(my_dp + j, n_dp)
        pltpu.make_async_remote_copy(
            src_ref=dp_rows.at[other], dst_ref=dp_rows.at[other],
            send_sem=d_send.at[j], recv_sem=d_recv.at[other],
            device_id={"dp": other}, device_id_type=MESH,
        ).wait_recv()
    total = dp_rows[0]
    for j in range(1, n_dp):
        total = total + dp_rows[j]
    dsink_ref[...] = total * (1.0 / math.sqrt(n_dp * n_ctx * tok))

    for dist in range(1, most):
        @pl.when(me + dist < n_ctx)
        def _():
            seg_copy(dist).wait_send()
    for h in range(KV_HEADS):
        for parity in (0, 1):
            for index, (held, step, kept) in enumerate(edges[parity]):
                @pl.when((odd == parity) & edge_live(held, step))
                def _():
                    forward(h, parity, index).wait_send()
            for held in range(1, most):
                p, index = parent_edge(parity, held)
                @pl.when((odd == parity) & (me >= held))
                def _():
                    backward(h, held, p, index).wait_send()
    for j in range(1, n_ctx):
        ctx_copy(j).wait_send()
    for j in range(1, n_dp):
        dp_copy(j).wait_send()


def body(n_dp, n_ctx, queries, key_rows, value_rows, cotangent, sink_logits, run_lengths, segment_ids):
    tok = queries.shape[1]
    most = min(8, n_ctx // 2)
    n_edges = max(len(part) for part in edge_lists(most).values())
    span = most * tok
    vmem = pl.BlockSpec(memory_space=pltpu.VMEM)
    smem = pl.BlockSpec(memory_space=pltpu.SMEM)
    like = lambda array: jax.ShapeDtypeStruct(array.shape, array.dtype)
    dma = pltpu.SemaphoreType.DMA
    flops = 12 * HEADS * tok * span * HEAD_DIM
    outs = pl.pallas_call(
        functools.partial(kernel, n_dp, n_ctx, most),
        out_shape=(
            like(queries), like(queries), like(key_rows), like(value_rows),
            jax.ShapeDtypeStruct((1, 128), jnp.float32),
        ),
        in_specs=[smem, smem] + [vmem] * 5,
        out_specs=[vmem] * 5,
        scratch_shapes=[
            pltpu.VMEM((KV_HEADS, 2, span, HEAD_DIM), jnp.bfloat16),
            pltpu.VMEM((KV_HEADS, 2, span, HEAD_DIM), jnp.float32),
            pltpu.VMEM((KV_HEADS, 2, span, HEAD_DIM), jnp.bfloat16),
            pltpu.VMEM((KV_HEADS, n_edges, 2, tok, HEAD_DIM), jnp.bfloat16),
            pltpu.VMEM((most, 1, tok), jnp.int32),
            pltpu.VMEM((span, tok), jnp.float32),
            pltpu.VMEM((HEADS, tok), jnp.float32),
            pltpu.VMEM((n_ctx, 1, 128), jnp.float32),
            pltpu.VMEM((n_dp, 1, 128), jnp.float32),
            dma((KV_HEADS, n_edges)), dma((KV_HEADS, most)),
            dma((KV_HEADS, most)), dma((KV_HEADS, n_edges)),
            dma((most,)), dma((most,)),
            dma((n_ctx,)), dma((n_ctx,)), dma((n_dp,)), dma((n_dp,)),
        ],
        compiler_params=pltpu.CompilerParams(
            collective_id=0, has_side_effects=True, vmem_limit_bytes=48 * 1024 * 1024
        ),
        cost_estimate=pl.CostEstimate(
            flops=flops, bytes_accessed=5 * tok * HEADS * HEAD_DIM * 2, transcendentals=HEADS * tok * span
        ),
    )(sink_logits, run_lengths, queries, key_rows, value_rows, cotangent, segment_ids)
    return (*outs[:4], outs[4][0, :HEADS])


def solution(mesh):
    rows = P("dp", "ctx", None)
    return jax.shard_map(
        functools.partial(body, mesh.shape["dp"], mesh.shape["ctx"]),
        mesh=mesh,
        in_specs=(rows, rows, rows, rows, P(), P("dp", None), P("dp", "ctx")),
        out_specs=(rows, rows, rows, rows, P()),
        check_vma=False,
    )
```

```python
import functools
import math

import jax
import jax.numpy as jnp
from jax import lax
from jax.experimental import pallas as pl
from jax.experimental.pallas import tpu as pltpu
from jax.sharding import PartitionSpec as P

HEADS = 16
KV_HEADS = 4
HEAD_DIM = 128
GROUP = HEADS // KV_HEADS
LOG2E = math.log2(math.e)
AWAY = -1e30
AHEAD = 4
VMEM_BYTES = 64 * 1024 * 1024
MESH = pl.DeviceIdType.MESH


def edge_lists(most):
    edges = {0: [], 1: []}
    for parity in (0, 1):
        for kept in range(1, most):
            step = 1 if kept == 1 or kept == 3 and parity == 1 else 2
            sender = parity if step % 2 == 0 else 1 - parity
            edges[sender].append((kept - step, step, kept))
    return edges


def levels(edges, most):
    depth = {(0, 0): 0, (1, 0): 0}
    while len(depth) < 2 * most:
        for parity in (0, 1):
            for held, step, kept in edges[parity]:
                if (parity, held) in depth:
                    depth[((parity + step) % 2, kept)] = depth[(parity, held)] + 1
    return depth


def kernel(
    n_dp, n_ctx, most,
    sink_hbm, runs_hbm, q_hbm, k_ref, v_ref, do_hbm, seg_hbm,
    att_ref, dq_ref, dk_ref, dv_ref, dsink_ref,
    kv, gsum, gout, gin, segs, bias, sink_rows, ctx_rows, dp_rows,
    q_ref, do_ref, sink_ref, runs_ref, i_sem, kv_sem,
    f_send, f_recv, b_send, b_recv, s_send, s_recv, c_send, c_recv, d_send, d_recv,
):
    tok = k_ref.shape[1]
    me = lax.axis_index("ctx")
    my_dp = lax.axis_index("dp")
    odd = lax.rem(me, 2)
    edges = edge_lists(most)
    depth = levels(edges, most)
    deepest = max(depth.values())
    factor = HEAD_DIM ** (-0.5)

    barrier = pltpu.get_barrier_semaphore()
    for j in range(1, n_ctx):
        pl.semaphore_signal(barrier, inc=1, device_id={"ctx": lax.rem(me + j, n_ctx)}, device_id_type=MESH)
    for j in range(1, n_dp):
        pl.semaphore_signal(barrier, inc=1, device_id={"dp": lax.rem(my_dp + j, n_dp)}, device_id_type=MESH)
    own = []
    for h in range(KV_HEADS):
        cols = pl.ds(h * HEAD_DIM, HEAD_DIM)
        own.append([
            pltpu.make_async_copy(ref.at[0, :, cols], kv.at[h, i, pl.ds(0, tok)], kv_sem.at[h, i])
            for i, ref in enumerate((k_ref, v_ref))
        ])
    loads = [
        pltpu.make_async_copy(source, target, i_sem.at[i])
        for i, (source, target) in enumerate([
            (seg_hbm, segs.at[0]), (runs_hbm, runs_ref), (sink_hbm, sink_ref),
            (q_hbm, q_ref), (do_hbm, do_ref),
        ])
    ]
    for copy in [loads[0]] + sum(own, []) + loads[1:]:
        copy.start()
    pl.semaphore_wait(barrier, n_ctx - 1 + n_dp - 1)

    def rows(dist):
        return pl.ds(dist * tok, tok)

    def forward(h, parity, index):
        held, step, kept = edges[parity][index]
        return pltpu.make_async_remote_copy(
            src_ref=kv.at[h, :, rows(held)],
            dst_ref=kv.at[h, :, rows(kept)],
            send_sem=f_send.at[h, index],
            recv_sem=f_recv.at[h, kept],
            device_id={"ctx": me + step},
            device_id_type=MESH,
        )

    def backward(h, kept, parity, index):
        held, step, k = edges[parity][index]
        return pltpu.make_async_remote_copy(
            src_ref=gout.at[h, :, rows(kept)],
            dst_ref=gin.at[h, index],
            send_sem=b_send.at[h, kept],
            recv_sem=b_recv.at[h, index],
            device_id={"ctx": me - step},
            device_id_type=MESH,
        )

    def edge_live(held, step):
        return (me >= held) & (me + step >= 0) & (me + step < n_ctx)

    def start_forward(h, level):
        for parity in (0, 1):
            for index, (held, step, kept) in enumerate(edges[parity]):
                if depth[(parity, held)] == level:
                    @pl.when((odd == parity) & edge_live(held, step))
                    def _():
                        forward(h, parity, index).start()

    def wait_forward(h, level):
        for kept in range(1, most):
            for parity in (0, 1):
                if depth[(parity, kept)] == level:
                    @pl.when((odd == parity) & (me >= kept))
                    def _():
                        pltpu.make_async_remote_copy(
                            src_ref=kv.at[h, :, rows(kept)],
                            dst_ref=kv.at[h, :, rows(kept)],
                            send_sem=f_send.at[h, 0],
                            recv_sem=f_recv.at[h, kept],
                            device_id={"ctx": lax.rem(me + 1, n_ctx)},
                            device_id_type=MESH,
                        ).wait_recv()

    def parent_edge(parity, kept):
        for p in (0, 1):
            for index, (held, step, k) in enumerate(edges[p]):
                if k == kept and (p + step) % 2 == parity:
                    return p, index

    def child_level(parity, held):
        below = [
            child_level((parity + step) % 2, kept) + 1
            for h0, step, kept in edges[parity] if h0 == held
        ]
        return max(below, default=0)

    def back_step(h, level):
        for parity in (0, 1):
            for held in range(most):
                if child_level(parity, held) != level:
                    continue
                for index, (h0, step, kept) in enumerate(edges[parity]):
                    if h0 == held:
                        @pl.when((odd == parity) & edge_live(held, step))
                        def _():
                            pltpu.make_async_remote_copy(
                                src_ref=gin.at[h, index],
                                dst_ref=gin.at[h, index],
                                send_sem=b_send.at[h, 0],
                                recv_sem=b_recv.at[h, index],
                                device_id={"ctx": lax.rem(me + 1, n_ctx)},
                                device_id_type=MESH,
                            ).wait_recv()
                            gsum[h, :, rows(held)] += gin[h, index].astype(jnp.float32)
                if held == 0:
                    @pl.when(odd == parity)
                    def _():
                        cols = slice(h * HEAD_DIM, (h + 1) * HEAD_DIM)
                        dk_ref[0, :, cols] = gsum[h, 0, 0:tok].astype(dk_ref.dtype)
                        dv_ref[0, :, cols] = gsum[h, 1, 0:tok].astype(dv_ref.dtype)
                else:
                    p, index = parent_edge(parity, held)
                    @pl.when((odd == parity) & (me >= held))
                    def _():
                        gout[h, :, rows(held)] = gsum[h, :, rows(held)].astype(gout.dtype)
                        backward(h, held, p, index).start()

    def seg_copy(dist):
        return pltpu.make_async_remote_copy(
            src_ref=segs.at[0], dst_ref=segs.at[dist],
            send_sem=s_send.at[dist], recv_sem=s_recv.at[dist],
            device_id={"ctx": me + dist}, device_id_type=MESH,
        )

    def start_own(h):
        for copy in own[h]:
            copy.wait()
        start_forward(h, 0)

    start_own(0)
    loads[0].wait()
    for dist in range(1, most):
        @pl.when(me + dist < n_ctx)
        def _():
            seg_copy(dist).start()
    for h in range(1, AHEAD):
        start_own(h)
    for copy in loads[1:]:
        copy.wait()

    for dist in range(1, most):
        @pl.when(me < dist)
        def _():
            kv[:, :, rows(dist), :] = jnp.zeros((KV_HEADS, 2, tok, HEAD_DIM), kv.dtype)
            segs[dist] = jnp.full(segs.shape[1:], -1, segs.dtype)

    for dist in range(1, most):
        @pl.when(me >= dist)
        def _():
            seg_copy(dist).wait_recv()

    def traj(shard):
        end, count = 0, 0
        for i in range(runs_ref.shape[1]):
            end = end + runs_ref[0, i]
            count = count + jnp.where(end <= shard, 1, 0)
        return count

    mine = traj(me)
    seg_query = jnp.broadcast_to(segs[0], (tok, tok))
    for dist in range(most):
        seg_key = jnp.transpose(jnp.broadcast_to(segs[dist], (tok, tok)).astype(jnp.float32))
        level = jnp.where((traj(me - dist) == mine) & (me >= dist), 0.0, AWAY)
        allowed = seg_key == seg_query.astype(jnp.float32)
        if dist == 0:
            key_pos = lax.broadcasted_iota(jnp.int32, (tok, tok), 0)
            query_pos = lax.broadcasted_iota(jnp.int32, (tok, tok), 1)
            allowed = allowed & (key_pos <= query_pos)
        bias[rows(dist), :] = jnp.where(allowed, level, AWAY)

    def nn(a, b):
        return jnp.dot(a, b, preferred_element_type=jnp.float32)

    def compute(h):
        heads = [h * GROUP + g for g in range(GROUP)]
        keys, values = kv[h, 0], kv[h, 1]
        keys_t, values_t = keys.T, values.T
        gk = gv = None
        for g in range(GROUP):
            cols = slice(heads[g] * HEAD_DIM, (heads[g] + 1) * HEAD_DIM)
            q = q_ref[0, :, cols]
            do = do_ref[0, :, cols]
            do_t = do.T
            scores = nn(keys, q.T) * (factor * LOG2E) + bias[...]
            sink = sink_ref[heads[g]] * LOG2E
            top = jnp.maximum(jnp.max(scores, axis=0, keepdims=True), sink)
            terms = jnp.exp2(scores - top)
            sink_exp = jnp.exp2(sink - top)
            denom = jnp.sum(terms, axis=0, keepdims=True) + sink_exp
            inv = 1.0 / denom
            weights = terms * inv
            low = weights.astype(jnp.bfloat16)
            att = nn(values_t, low).astype(jnp.bfloat16)
            att_ref[0, :, cols] = att.T
            row_dot = jnp.sum(att.astype(jnp.float32) * do_t.astype(jnp.float32), axis=0, keepdims=True)
            gw = nn(values, do_t)
            gs = (weights * (gw - row_dot)).astype(jnp.bfloat16)
            gq = nn(keys_t, gs) * factor
            dq_ref[0, :, cols] = gq.astype(jnp.bfloat16).T
            new_k, new_v = nn(gs, q), nn(low, do)
            gk = new_k if gk is None else gk + new_k
            gv = new_v if gv is None else gv + new_v
            sink_rows[pl.ds(heads[g], 1), :] = -(sink_exp * inv * row_dot)
        gsum[h, 0] = gk * factor
        gsum[h, 1] = gv

    def run_forward(upto):
        for h, level in upto:
            wait_forward(h, level)
            if level < deepest:
                start_forward(h, level)
            if level == 1 and h + AHEAD < KV_HEADS:
                start_own(h + AHEAD)

    order = sorted(
        ((h, level) for h in range(KV_HEADS) for level in range(1, deepest + 1)),
        key=lambda item: (item[0] + item[1], item[0]),
    )
    done = 0
    back_deepest = max(child_level(p, k) for p in (0, 1) for k in range(most))
    pending = []
    for h in range(KV_HEADS):
        last = sum(other + level <= h + deepest for other, level in order)
        run_forward(order[done:last])
        done = max(done, last)
        compute(h)
        back_step(h, 0)
        for other in range(h):
            level = h - other
            if level <= back_deepest:
                back_step(other, level)
                pending.append((other, level))

    padded = jnp.concatenate(
        [sink_rows[...], jnp.zeros((128 - HEADS, tok), jnp.float32)], 0
    )
    ctx_rows[me] = jnp.sum(padded.T, axis=0, keepdims=True)

    def ctx_copy(j):
        return pltpu.make_async_remote_copy(
            src_ref=ctx_rows.at[me], dst_ref=ctx_rows.at[me],
            send_sem=c_send.at[j], recv_sem=c_recv.at[me],
            device_id={"ctx": lax.rem(me + j, n_ctx)}, device_id_type=MESH,
        )

    def dp_copy(j):
        return pltpu.make_async_remote_copy(
            src_ref=dp_rows.at[my_dp], dst_ref=dp_rows.at[my_dp],
            send_sem=d_send.at[j], recv_sem=d_recv.at[my_dp],
            device_id={"dp": lax.rem(my_dp + j, n_dp)}, device_id_type=MESH,
        )

    for j in range(1, n_ctx):
        ctx_copy(j).start()

    rest = sorted(
        ((h, level) for h in range(KV_HEADS) for level in range(1, back_deepest + 1)
         if (h, level) not in pending),
        key=lambda item: (item[0] + item[1], item[0]),
    )
    half = [item for item in rest if item != (KV_HEADS - 1, back_deepest)]
    for h, level in half:
        back_step(h, level)

    for j in range(1, n_ctx):
        other = lax.rem(me + j, n_ctx)
        pltpu.make_async_remote_copy(
            src_ref=ctx_rows.at[other], dst_ref=ctx_rows.at[other],
            send_sem=c_send.at[j], recv_sem=c_recv.at[other],
            device_id={"ctx": other}, device_id_type=MESH,
        ).wait_recv()
    total = ctx_rows[0]
    for j in range(1, n_ctx):
        total = total + ctx_rows[j]
    dp_rows[my_dp] = total
    for j in range(1, n_dp):
        dp_copy(j).start()

    for item in rest:
        if item not in half:
            back_step(*item)

    for j in range(1, n_dp):
        other = lax.rem(my_dp + j, n_dp)
        pltpu.make_async_remote_copy(
            src_ref=dp_rows.at[other], dst_ref=dp_rows.at[other],
            send_sem=d_send.at[j], recv_sem=d_recv.at[other],
            device_id={"dp": other}, device_id_type=MESH,
        ).wait_recv()
    total = dp_rows[0]
    for j in range(1, n_dp):
        total = total + dp_rows[j]
    dsink_ref[...] = total * (1.0 / math.sqrt(n_dp * n_ctx * tok))

    for dist in range(1, most):
        @pl.when(me + dist < n_ctx)
        def _():
            seg_copy(dist).wait_send()
    for h in range(KV_HEADS):
        for parity in (0, 1):
            for index, (held, step, kept) in enumerate(edges[parity]):
                @pl.when((odd == parity) & edge_live(held, step))
                def _():
                    forward(h, parity, index).wait_send()
            for held in range(1, most):
                p, index = parent_edge(parity, held)
                @pl.when((odd == parity) & (me >= held))
                def _():
                    backward(h, held, p, index).wait_send()
    for j in range(1, n_ctx):
        ctx_copy(j).wait_send()
    for j in range(1, n_dp):
        dp_copy(j).wait_send()


def body(n_dp, n_ctx, queries, key_rows, value_rows, cotangent, sink_logits, run_lengths, segment_ids):
    tok = queries.shape[1]
    most = min(8, n_ctx // 2)
    n_edges = max(len(part) for part in edge_lists(most).values())
    span = most * tok
    vmem = pl.BlockSpec(memory_space=pltpu.VMEM)
    hbm = pl.BlockSpec(memory_space=pltpu.HBM)
    like = lambda array: jax.ShapeDtypeStruct(array.shape, array.dtype)
    dma = pltpu.SemaphoreType.DMA
    flops = 12 * HEADS * tok * span * HEAD_DIM
    outs = pl.pallas_call(
        functools.partial(kernel, n_dp, n_ctx, most),
        out_shape=(
            like(queries), like(queries), like(key_rows), like(value_rows),
            jax.ShapeDtypeStruct((1, 128), jnp.float32),
        ),
        in_specs=[hbm] * 7,
        out_specs=[vmem] * 5,
        scratch_shapes=[
            pltpu.VMEM((KV_HEADS, 2, span, HEAD_DIM), jnp.bfloat16),
            pltpu.VMEM((KV_HEADS, 2, span, HEAD_DIM), jnp.float32),
            pltpu.VMEM((KV_HEADS, 2, span, HEAD_DIM), jnp.bfloat16),
            pltpu.VMEM((KV_HEADS, n_edges, 2, tok, HEAD_DIM), jnp.bfloat16),
            pltpu.VMEM((most, 1, tok), jnp.int32),
            pltpu.VMEM((span, tok), jnp.float32),
            pltpu.VMEM((HEADS, tok), jnp.float32),
            pltpu.VMEM((n_ctx, 1, 128), jnp.float32),
            pltpu.VMEM((n_dp, 1, 128), jnp.float32),
            pltpu.VMEM(queries.shape, queries.dtype), pltpu.VMEM(cotangent.shape, cotangent.dtype),
            pltpu.SMEM(sink_logits.shape, jnp.float32), pltpu.SMEM(run_lengths.shape, jnp.int32),
            dma((5,)), dma((KV_HEADS, 2)),
            dma((KV_HEADS, n_edges)), dma((KV_HEADS, most)),
            dma((KV_HEADS, most)), dma((KV_HEADS, n_edges)),
            dma((most,)), dma((most,)),
            dma((n_ctx,)), dma((n_ctx,)), dma((n_dp,)), dma((n_dp,)),
        ],
        compiler_params=pltpu.CompilerParams(
            collective_id=0, has_side_effects=True, vmem_limit_bytes=VMEM_BYTES
        ),
        cost_estimate=pl.CostEstimate(
            flops=flops, bytes_accessed=5 * tok * HEADS * HEAD_DIM * 2, transcendentals=HEADS * tok * span
        ),
    )(sink_logits, run_lengths, queries, key_rows, value_rows, cotangent, segment_ids)
    return (*outs[:4], outs[4][0, :HEADS])


def solution(mesh):
    rows = P("dp", "ctx", None)
    return jax.shard_map(
        functools.partial(body, mesh.shape["dp"], mesh.shape["ctx"]),
        mesh=mesh,
        in_specs=(rows, rows, rows, rows, P(), P("dp", None), P("dp", "ctx")),
        out_specs=(rows, rows, rows, rows, P()),
        check_vma=False,
    )
```
